32 devices in a mesh: group: 2 (over y), blk: 4 (over x, core), rep: 4 (over z).
Axes of the slice: x: 2, y: 2, z: 4, core: 2. Of those that a mesh axis runs over, the one named last changes fastest.
Arguments:
- feats: bfloat16 [12288, 128], P(('group', 'blk')), parts along dimension 0, may hold values from -6 to 6
- tiles: bfloat16 [96, 24, 128, 128], P(('group', 'blk'), None, 'rep'), parts along dimension 0, may hold values from -0.109375 to 0.109375
- col_local: int32 [96, 24], P(('group', 'blk')), parts along dimension 0, may hold values from 0 to 11, as said below
- tile_count: int32 [96, 4], P(('group', 'blk')), parts along dimension 0, may hold values from 0 to 6, as said below
- w_self: bfloat16 [2, 128, 128], replicated, may hold values from -0.5 to 0.5
- w_neigh: bfloat16 [2, 128, 128], replicated, may hold values from -0.5 to 0.5
- bias: float32 [2, 128], replicated, may hold values from -3 to 3
- cotangent: bfloat16 [12288, 128], P(('group', 'blk')), parts along dimension 0, may hold values from -0.076171875 to 0.076171875
Outputs:
- logits: bfloat16 [12288, 128], P(('group', 'blk')), parts along dimension 0
- grad_self: float32 [4, 128, 128], P('group'), parts along dimension 0
- grad_neigh: float32 [4, 128, 128], P('group'), parts along dimension 0
- grad_bias: float32 [4, 128], P('group'), parts along dimension 0
The draws below stay inside these ranges and needn't reach their ends.
There are 2 independent parts, one for each index of `group`. The reference program is written for one: setup_inputs(seed, part) draws one part's arguments, and reference() takes and returns one part's arrays. A program takes and returns all parts, laid end to end along the dimension named above; an argument that names none is the same for every part. Nothing has to cross between parts.
Inputs may be any that keep to these rules, and one draw needn't show every extreme that they name: `col_local`: the column block of a slot is one of the 12 row blocks held by that slot's source index of blk; the 6 slots of one row block and one source name distinct column blocks. The live tiles are the first tile_count slots of each group of 6; some entry equals 6.
All inputs are finite; a program needn't handle non-finite values.
Results may differ from the reference program's by a relative error of at most 0.0062.
Values may be sent and summed in bfloat16 or wider, within the bound.
A program may use at most 64 MiB of HBM per device.

```python
import jax
import jax.numpy as jnp
from jax import lax

FEAT = 128
TILE = 128
ROWB = 12
KS = 6
LAYERS = 2
NRB = 48
NODES = 6144
SLOTS = 24
N_BLK = 4


def draw_col_local(key, part):
    key = jax.random.fold_in(key, 11)
    scores = jax.random.randint(key, (ROWB * N_BLK, N_BLK, ROWB), 0, 1 << 20) * ROWB + jnp.arange(ROWB, dtype=jnp.int32)[None, None, :]
    order = jnp.argsort(scores, axis=-1)
    picked = order[:, :, :KS]
    picked = picked.at[0, 0].set(jnp.arange(ROWB - KS, ROWB, dtype=jnp.int32))
    picked = picked.at[0, N_BLK - 1].set(jnp.arange(KS, dtype=jnp.int32))
    return picked.reshape(ROWB * N_BLK, N_BLK * KS).astype(jnp.int32)


def draw_tile_count(key, part):
    key = jax.random.fold_in(key, 7)
    first_key, second_key = jax.random.split(key)
    base = jax.random.randint(first_key, (ROWB * N_BLK, N_BLK), 0, KS + 1)
    heavy = jax.random.randint(second_key, (ROWB * N_BLK, 1), 0, 4) == 0
    counts = jnp.where(heavy, KS, base)
    counts = counts.at[0, 0].set(KS)
    return counts.astype(jnp.int32)


def block_scale(stream_key, shape, shards, low, top_value):
    def one(axis_at, blocks):
        steps = jax.random.uniform(jax.random.fold_in(jax.random.fold_in(stream_key, 6), axis_at), (blocks,), jnp.float32, low / len(shards), top_value / len(shards))
        return jnp.repeat(jnp.exp(steps), shape[axis_at] // blocks).reshape((-1,) + (1,) * (len(shape) - axis_at - 1))

    level = one(*shards[0])
    for cut in shards[1:]:
        level = level * one(*cut)
    return level


def centred(rng, dims, deviation, most, pieces=(), held_as=jnp.bfloat16):
    values = jax.random.normal(rng, dims, jnp.float32) * deviation
    if len(pieces) > 0:
        values = block_scale(rng, dims, pieces, -0.22, 0.18) * values
    return jnp.clip(values, min=-most, max=most).astype(held_as)


def setup_inputs(seed: int = 0, part: int = 0) -> dict:
    streams_of = jax.random.split(jax.random.key(seed), 9)
    part_splits = jax.random.split(jax.random.fold_in(streams_of[8], part), 9)
    return {
        "feats": centred(part_splits[0], (NODES, FEAT), 1.0, 6.0, ((0, 4),)),
        "tiles": centred(part_splits[1], (NRB, SLOTS, TILE, TILE), (TILE * N_BLK * KS) ** -0.5, 0.109375, ((0, 4), (2, 4))),
        "col_local": draw_col_local(jax.random.fold_in(jax.random.fold_in(streams_of[8], part), 71), part),
        "tile_count": draw_tile_count(jax.random.fold_in(jax.random.fold_in(streams_of[8], part), 71), part),
        "w_self": centred(streams_of[4], (LAYERS, FEAT, FEAT), FEAT ** -0.5, 0.5),
        "w_neigh": centred(streams_of[5], (LAYERS, FEAT, FEAT), FEAT ** -0.5, 0.5),
        "bias": centred(streams_of[6], (LAYERS, FEAT), 0.5, 3.0, (), jnp.float32),
        "cotangent": centred(part_splits[7], (NODES, FEAT), (1.0 / (ROWB * TILE * N_BLK) ** 0.5), 0.076171875, ((0, 4),)),
    }


def slot_tables(col_local, tile_count):
    slot_total = col_local.shape[1]
    index = jnp.arange(slot_total, dtype=jnp.int32)
    source = index // KS
    column = (source[None, :] * ROWB + col_local).astype(jnp.int32)
    alive = (index % KS)[None, :] < jnp.take(tile_count, source, axis=1)
    return column, alive


def aggregate(hidden, tiles, column, alive):
    blocks = hidden.reshape(-1, TILE, FEAT)

    def one_row(items):
        tile_row, column_row, alive_row = items
        gathered = blocks[column_row].astype(jnp.float32) * alive_row[:, None, None].astype(jnp.float32)
        return jnp.einsum('mji,mjf->if', tile_row.astype(jnp.float32), gathered)

    return lax.map(one_row, (tiles, column, alive)).reshape(-1, FEAT)


def transpose_aggregate(grad_rows, tiles, column, alive):
    blocks = grad_rows.reshape(-1, TILE, FEAT).astype(jnp.float32)

    def one_row(carry, items):
        tile_row, column_row, alive_row, grad_block = items
        product = jnp.einsum('mji,if->mjf', tile_row.astype(jnp.float32), grad_block)
        product = product * alive_row[:, None, None].astype(jnp.float32)
        return carry.at[column_row].add(product), None

    start_value = jnp.zeros(blocks.shape, jnp.float32)
    result, _ = lax.scan(one_row, start_value, (tiles, column, alive, blocks))
    return result.reshape(-1, FEAT)


def reference(feats, tiles, col_local, tile_count, w_self, w_neigh, bias, cotangent):
    column, alive = slot_tables(col_local, tile_count)
    agg0 = aggregate(feats, tiles, column, alive).astype(jnp.bfloat16)
    z0 = jnp.dot(feats, w_self[0], preferred_element_type=jnp.float32) + jnp.dot(agg0, w_neigh[0], preferred_element_type=jnp.float32) + bias[0]
    h1 = jax.nn.silu(z0).astype(jnp.bfloat16)
    agg1 = aggregate(h1, tiles, column, alive).astype(jnp.bfloat16)
    z1 = jnp.dot(h1, w_self[1], preferred_element_type=jnp.float32) + jnp.dot(agg1, w_neigh[1], preferred_element_type=jnp.float32) + bias[1]
    logits = z1.astype(jnp.bfloat16)
    back1 = jnp.dot(cotangent, w_neigh[1].T, preferred_element_type=jnp.float32).astype(jnp.bfloat16)
    spread = transpose_aggregate(back1, tiles, column, alive)
    dh1 = (jnp.dot(cotangent, w_self[1].T, preferred_element_type=jnp.float32) + spread).astype(jnp.bfloat16)
    sigma = jax.nn.sigmoid(z0)
    dz0 = (dh1.astype(jnp.float32) * sigma * (1.0 + z0 * (1.0 - sigma))).astype(jnp.bfloat16)
    self_zero = jnp.dot(feats.T, dz0, preferred_element_type=jnp.float32)
    self_one = jnp.dot(h1.T, cotangent, preferred_element_type=jnp.float32)
    neigh_zero = jnp.dot(agg0.T, dz0, preferred_element_type=jnp.float32)
    neigh_one = jnp.dot(agg1.T, cotangent, preferred_element_type=jnp.float32)
    bias_zero = jnp.sum(dz0.astype(jnp.float32), axis=0)
    bias_one = jnp.sum(cotangent.astype(jnp.float32), axis=0)
    return (logits, jnp.stack([self_zero, self_one]), jnp.stack([neigh_zero, neigh_one]), jnp.stack([bias_zero, bias_one]))
```

```python
import functools

import jax
import jax.numpy as jnp
from jax import lax
from jax.experimental import pallas as pl
from jax.experimental.pallas import tpu as pltpu
from jax.sharding import PartitionSpec as P

MESH = pl.DeviceIdType.MESH
F32 = jnp.float32
BF16 = jnp.bfloat16


def contract(a, b, a_dim, b_dim):
    return lax.dot_general(a, b, (((a_dim,), (b_dim,)), ((), ())), preferred_element_type=F32)


def kernel(
    n_blk,
    n_rep,
    feats,
    tiles,
    col_local,
    tile_count,
    w_self,
    w_neigh,
    bias,
    cot,
    logits,
    grad_self,
    grad_neigh,
    grad_bias,
    dense,
    dense_t,
    z0_keep,
    agg_keep,
    x_in,
    spread_out,
    spread_in,
    agg_out,
    agg_in,
    logits_in,
    part_a,
    part_b,
    blk_in_a,
    blk_in_b,
    half_a,
    half_b,
    rep_in_a,
    rep_in_b,
    full_a,
    full_b,
    x_send,
    x_recv,
    spread_send,
    spread_recv,
    agg_send,
    agg_recv,
    logits_send,
    logits_recv,
    grad_send,
    grad_recv,
):
    row_blocks, slots, share, edge = tiles.shape
    slot_count = slots // n_blk
    width = feats.shape[-1]
    rows = row_blocks * share
    nodes = row_blocks * edge
    piece = width // n_blk
    blk = lax.axis_index("blk")
    rep = lax.axis_index("rep")
    whole_tiles = share % 16 == 0

    def flat(value):
        if whole_tiles:
            return value.reshape(-1, value.shape[-1]).astype(BF16)
        return value.astype(F32).reshape(-1, value.shape[-1]).astype(BF16)

    def blocks_of(value):
        if whole_tiles:
            return value.reshape(row_blocks, share, width)
        return value.astype(F32).reshape(row_blocks, share, width).astype(BF16)

    sends = []

    def send(source, target, send_sem, recv_sem, axis, partner):
        copy = pltpu.make_async_remote_copy(
            src_ref=source,
            dst_ref=target,
            send_sem=send_sem,
            recv_sem=recv_sem,
            device_id={axis: partner},
            device_id_type=MESH,
        )
        copy.start()
        sends.append(copy)
        return copy

    blk_to = [lax.rem(blk + d, n_blk) for d in range(n_blk)]
    rep_to = [lax.rem(rep + d, n_rep) for d in range(n_rep)]

    barrier = pltpu.get_barrier_semaphore()
    for d in range(1, n_blk):
        pl.semaphore_signal(barrier, inc=1, device_id={"blk": blk_to[d]}, device_id_type=MESH)
    for d in range(1, n_rep):
        pl.semaphore_signal(barrier, inc=1, device_id={"rep": rep_to[d]}, device_id_type=MESH)

    feats_share = flat(feats[:, rep])
    cot_share = flat(cot[:, rep])
    x_in[0, blk] = feats_share
    pl.semaphore_wait(barrier, n_blk - 1 + n_rep - 1)

    def share_out(layer):
        mine = x_in.at[layer, blk]
        return [
            send(mine, mine, x_send.at[layer, d], x_recv.at[layer, d], "blk", blk_to[d])
            for d in range(1, n_blk)
        ]

    arriving = share_out(0)

    unit_row = lax.broadcasted_iota(jnp.int32, (edge, edge), 0)
    unit_col = lax.broadcasted_iota(jnp.int32, (edge, edge), 1)
    unit = jnp.where(unit_row == unit_col, 1.0, 0.0).astype(BF16)

    @pl.loop(0, row_blocks)
    def _(r):
        lanes = pl.ds(pl.multiple_of(r * edge, edge), edge)
        for s in range(n_blk):
            count = tile_count[r, s]
            named = [
                jnp.where(k < count, col_local[r, s * slot_count + k], -1)
                for k in range(slot_count)
            ]
            for c in range(row_blocks):
                slot = jnp.int32(-1)
                for k in range(slot_count):
                    slot = jnp.where(named[k] == c, s * slot_count + k, slot)
                tile = tiles[r, jnp.maximum(slot, 0)].astype(dense.dtype)
                dense[s * row_blocks + c, :, lanes] = jnp.where(slot >= 0, tile, jnp.zeros_like(tile))
        turned = contract(unit, flat(dense[:, :, lanes]), 1, 1).astype(dense_t.dtype)
        for q in range(n_rep):
            dense_t[q, r] = turned[q * share : (q + 1) * share]

    def aggregate(layer, arriving):
        for copy in arriving:
            copy.wait_recv()
        x = x_in[layer].reshape(n_blk * rows, width)

        copies = []
        for d in range(1, n_rep):
            part = jnp.dot(flat(dense_t[rep_to[d]]), x, preferred_element_type=F32)
            agg_out[layer, d - 1] = part.astype(BF16)
            copies.append(
                send(
                    agg_out.at[layer, d - 1],
                    agg_in.at[layer, d - 1],
                    agg_send.at[layer, d],
                    agg_recv.at[layer, d],
                    "rep",
                    rep_to[d],
                )
            )
        agg_keep[...] = jnp.dot(flat(dense_t[rep]), x, preferred_element_type=F32)
        return copies

    def finish_aggregate(layer, copies):
        total = agg_keep[...]
        for d, copy in enumerate(copies):
            copy.wait_recv()
            total = total + agg_in[layer, d].astype(F32)
        return total.astype(BF16)

    summing = aggregate(0, arriving)

    back = contract(flat(cot[...].reshape(row_blocks * n_rep, share, width)), w_neigh[1], 1, 1).astype(BF16)
    spreading = []
    for d in range(1, n_blk):
        to = dense[pl.ds(blk_to[d] * row_blocks, row_blocks)]
        spread_out[d - 1] = jnp.dot(flat(to), back, preferred_element_type=F32).astype(BF16)
        spreading.append(
            send(
                spread_out.at[d - 1],
                spread_in.at[d - 1],
                spread_send.at[d],
                spread_recv.at[d],
                "blk",
                blk_to[d],
            )
        )
    own = dense[pl.ds(blk * row_blocks, row_blocks)]
    hidden_grad = jnp.dot(flat(own), back, preferred_element_type=F32) + contract(
        cot_share, w_self[1], 1, 1
    )

    z0_part = jnp.dot(feats_share, w_self[0], preferred_element_type=F32) + bias[0:1]
    agg0 = finish_aggregate(0, summing)
    z0 = z0_part + jnp.dot(agg0, w_neigh[0], preferred_element_type=F32)
    sigma = 1.0 / (1.0 + jnp.exp(-z0))
    h1 = (z0 * sigma).astype(BF16)
    x_in[1, blk] = h1
    arriving = share_out(1)

    for d, copy in enumerate(spreading):
        copy.wait_recv()
        hidden_grad = hidden_grad + spread_in[d].astype(F32)
    dh1 = hidden_grad.astype(BF16).astype(F32)
    dz0 = (dh1 * sigma * (1.0 + z0 * (1.0 - sigma))).astype(BF16)

    def place(part, at, value):
        for q in range(n_blk):
            part[q, at * piece : (at + 1) * piece] = value[q * piece : (q + 1) * piece]

    place(part_a, 0, contract(feats_share, dz0, 0, 0))
    place(part_a, 1, contract(agg0, dz0, 0, 0))
    place(part_a, 2, contract(h1, cot_share, 0, 0))
    bias_rows = jnp.concatenate(
        [
            jnp.sum(dz0.astype(F32), axis=0, keepdims=True),
            jnp.sum(cot_share.astype(F32), axis=0, keepdims=True),
            jnp.zeros((6, width), F32),
        ],
        axis=0,
    )
    for q in range(n_blk):
        part_a[q, 3 * piece :] = bias_rows

    def scatter_blk(which, part, blk_in):
        return [
            send(
                part.at[blk_to[d]],
                blk_in.at[d - 1],
                grad_send.at[which, 0, d],
                grad_recv.at[which, 0, d],
                "blk",
                blk_to[d],
            )
            for d in range(1, n_blk)
        ]

    def swap_rep(which, part, blk_in, half, rep_in, copies):
        total = part[blk]
        for d, copy in enumerate(copies):
            copy.wait_recv()
            total = total + blk_in[d]
        half[...] = total
        return [
            send(
                half,
                rep_in.at[d - 1],
                grad_send.at[which, 1, d],
                grad_recv.at[which, 1, d],
                "rep",
                rep_to[d],
            )
            for d in range(1, n_rep)
        ]

    def gather_blk(which, half, rep_in, full, copies):
        for copy in copies:
            copy.wait_recv()
        rep_in[n_rep - 1] = half[...]

        def of(q):
            return rep_in[lax.rem(rep + 2 * n_rep - 1 - q, n_rep)]

        total = of(0)
        for q in range(1, n_rep):
            total = total + of(q)
        full[blk] = total
        return [
            send(
                full.at[blk],
                full.at[blk],
                grad_send.at[which, 2, d],
                grad_recv.at[which, 2, d],
                "blk",
                blk_to[d],
            )
            for d in range(1, n_blk)
        ]

    grads_a = scatter_blk(0, part_a, blk_in_a)

    summing = aggregate(1, arriving)
    grads_a = swap_rep(0, part_a, blk_in_a, half_a, rep_in_a, grads_a)
    z1_part = jnp.dot(h1, w_self[1], preferred_element_type=F32) + bias[1:2]

    agg1 = finish_aggregate(1, summing)
    z1 = z1_part + jnp.dot(agg1, w_neigh[1], preferred_element_type=F32)
    logits_in[rep] = z1.astype(BF16)
    gathering = [
        send(
            logits_in.at[rep],
            logits_in.at[rep],
            logits_send.at[d],
            logits_recv.at[d],
            "rep",
            rep_to[d],
        )
        for d in range(1, n_rep)
    ]
    place(part_b, 0, contract(agg1, cot_share, 0, 0))
    grads_b = scatter_blk(1, part_b, blk_in_b)
    grads_a = gather_blk(0, half_a, rep_in_a, full_a, grads_a)
    grads_b = swap_rep(1, part_b, blk_in_b, half_b, rep_in_b, grads_b)
    grads_b = gather_blk(1, half_b, rep_in_b, full_b, grads_b)

    for copy in grads_a:
        copy.wait_recv()
    for q in range(n_blk):
        at = slice(q * piece, (q + 1) * piece)
        grad_self[0, at] = full_a[q, 0:piece]
        grad_neigh[0, at] = full_a[q, piece : 2 * piece]
        grad_self[1, at] = full_a[q, 2 * piece : 3 * piece]
    grad_bias[...] = full_a[0, 3 * piece : 3 * piece + 2]

    for copy in grads_b:
        copy.wait_recv()
    for q in range(n_blk):
        grad_neigh[1, q * piece : (q + 1) * piece] = full_b[q]
    for copy in gathering:
        copy.wait_recv()
    for q in range(n_rep):
        logits[:, q] = blocks_of(logits_in[q])
    for copy in sends:
        copy.wait_send()


def solution(mesh):
    n_blk, n_rep = mesh.shape["blk"], mesh.shape["rep"]

    def shards(feats, tiles, col_local, tile_count, w_self, w_neigh, bias, cotangent):
        row_blocks, slots, share, edge = tiles.shape
        width = feats.shape[1]
        rows = row_blocks * share
        piece = width // n_blk
        held = BF16 if share % 16 == 0 else F32
        vmem = pl.BlockSpec(memory_space=pltpu.VMEM)
        smem = pl.BlockSpec(memory_space=pltpu.SMEM)
        split = (row_blocks, n_rep, share, width)
        dma = pltpu.SemaphoreType.DMA
        a_rows, b_rows = 3 * piece + 8, piece
        logits, grad_self, grad_neigh, grad_bias = pl.pallas_call(
            functools.partial(kernel, n_blk, n_rep),
            out_shape=(
                jax.ShapeDtypeStruct(split, BF16),
                jax.ShapeDtypeStruct((2, width, width), F32),
                jax.ShapeDtypeStruct((2, width, width), F32),
                jax.ShapeDtypeStruct((2, width), F32),
            ),
            in_specs=[vmem, vmem, smem, smem, vmem, vmem, vmem, vmem],
            out_specs=(vmem, vmem, vmem, vmem),
            scratch_shapes=[
                pltpu.VMEM((n_blk * row_blocks, share, row_blocks * edge), held),
                pltpu.VMEM((n_rep, row_blocks, share, n_blk * rows), held),
                pltpu.VMEM((rows, width), F32),
                pltpu.VMEM((rows, width), F32),
                pltpu.VMEM((2, n_blk, rows, width), BF16),
                pltpu.VMEM((n_blk - 1, rows, width), BF16),
                pltpu.VMEM((n_blk - 1, rows, width), BF16),
                pltpu.VMEM((2, n_rep - 1, rows, width), BF16),
                pltpu.VMEM((2, n_rep - 1, rows, width), BF16),
                pltpu.VMEM((n_rep, rows, width), BF16),
                pltpu.VMEM((n_blk, a_rows, width), F32),
                pltpu.VMEM((n_blk, b_rows, width), F32),
                pltpu.VMEM((n_blk - 1, a_rows, width), F32),
                pltpu.VMEM((n_blk - 1, b_rows, width), F32),
                pltpu.VMEM((a_rows, width), F32),
                pltpu.VMEM((b_rows, width), F32),
                pltpu.VMEM((n_rep, a_rows, width), F32),
                pltpu.VMEM((n_rep, b_rows, width), F32),
                pltpu.VMEM((n_blk, a_rows, width), F32),
                pltpu.VMEM((n_blk, b_rows, width), F32),
                dma((2, n_blk)),
                dma((2, n_blk)),
                dma((n_blk,)),
                dma((n_blk,)),
                dma((2, n_rep)),
                dma((2, n_rep)),
                dma((n_rep,)),
                dma((n_rep,)),
                dma((2, 3, max(n_blk, n_rep))),
                dma((2, 3, max(n_blk, n_rep))),
            ],
            compiler_params=pltpu.CompilerParams(
                collective_id=0, has_side_effects=True, vmem_limit_bytes=52 * 2**20
            ),
        )(
            feats.reshape(split),
            tiles,
            col_local,
            tile_count,
            w_self,
            w_neigh,
            bias,
            cotangent.reshape(split),
        )
        return logits.reshape(feats.shape), grad_self, grad_neigh, grad_bias

    return jax.shard_map(
        shards,
        mesh=mesh,
        in_specs=(
            P(("group", "blk"), None),
            P(("group", "blk"), None, "rep", None),
            P(("group", "blk"), None),
            P(("group", "blk"), None),
            P(),
            P(),
            P(),
            P(("group", "blk"), None),
        ),
        out_specs=(
            P(("group", "blk"), None),
            P("group", None, None),
            P("group", None, None),
            P("group", None),
        ),
        check_vma=False,
    )
```

```python
import functools

import jax
import jax.numpy as jnp
from jax import lax
from jax.experimental import pallas as pl
from jax.experimental.pallas import tpu as pltpu
from jax.sharding import PartitionSpec as P

MESH = pl.DeviceIdType.MESH
F32 = jnp.float32
BF16 = jnp.bfloat16
HALVES = 2


def contract(a, b, a_dim, b_dim):
    return lax.dot_general(a, b, (((a_dim,), (b_dim,)), ((), ())), preferred_element_type=F32)


def kernel(
    n_blk,
    n_rep,
    feats_hbm,
    tiles_hbm,
    col_hbm,
    count_hbm,
    w_self_hbm,
    w_neigh_hbm,
    bias_hbm,
    cot_hbm,
    logits,
    grad_self,
    grad_neigh,
    grad_bias,
    feats,
    tiles,
    col_local,
    tile_count,
    w_self,
    w_neigh,
    bias,
    cot,
    dense,
    dense_t,
    agg_keep,
    x_in,
    spread_out,
    spread_in,
    agg_out,
    agg_in,
    logits_in,
    part,
    blk_in,
    half,
    rep_in,
    full,
    load_sem,
    x_send,
    x_recv,
    spread_send,
    spread_recv,
    agg_send,
    agg_recv,
    logits_send,
    logits_recv,
    grad_send,
    grad_recv,
):
    row_blocks, slots, share, edge = tiles.shape
    slot_count = slots // n_blk
    width = feats.shape[-1]
    rows = row_blocks * share
    piece = width // n_blk
    n_chip = n_blk // 2
    half_blocks = row_blocks // HALVES
    half_rows = rows // HALVES
    blk = lax.axis_index("blk")
    rep = lax.axis_index("rep")
    whole_tiles = share % 16 == 0

    def flat(value):
        if whole_tiles:
            return value.reshape(-1, value.shape[-1]).astype(BF16)
        return value.astype(F32).reshape(-1, value.shape[-1]).astype(BF16)

    def blocks_of(value):
        if whole_tiles:
            return value.reshape(row_blocks, share, width)
        return value.astype(F32).reshape(row_blocks, share, width).astype(BF16)

    sends = []

    def send(source, target, send_sem, recv_sem, axis, partner):
        copy = pltpu.make_async_remote_copy(
            src_ref=source,
            dst_ref=target,
            send_sem=send_sem,
            recv_sem=recv_sem,
            device_id={axis: partner},
            device_id_type=MESH,
        )
        copy.start()
        sends.append(copy)
        return copy

    blk_to = [lax.rem(blk + d, n_blk) for d in range(n_blk)]
    rep_to = [lax.rem(rep + d, n_rep) for d in range(n_rep)]
    core = lax.rem(blk, 2)
    mate = blk + 1 - 2 * core

    barrier = pltpu.get_barrier_semaphore()
    for d in range(1, n_blk):
        pl.semaphore_signal(barrier, inc=1, device_id={"blk": blk_to[d]}, device_id_type=MESH)
    for d in range(1, n_rep):
        pl.semaphore_signal(barrier, inc=1, device_id={"rep": rep_to[d]}, device_id_type=MESH)

    pairs = [
        (feats_hbm, feats),
        (col_hbm, col_local),
        (count_hbm, tile_count),
        (tiles_hbm, tiles),
        (cot_hbm, cot),
        (w_self_hbm, w_self),
        (w_neigh_hbm, w_neigh),
        (bias_hbm, bias),
    ]
    loads = [pltpu.make_async_copy(a, b, load_sem.at[i]) for i, (a, b) in enumerate(pairs)]
    for load in loads:
        load.start()
    loads[0].wait()
    feats_share = flat(feats[:, rep])
    x_in[0, blk] = feats_share
    pl.semaphore_wait(barrier, n_blk - 1 + n_rep - 1)

    def span(h):
        return pl.ds(h * half_rows, half_rows)

    def share_out(layer, h):
        mine = x_in.at[layer, blk, span(h)]
        out = []
        for d in range(1, n_chip):
            to = lax.rem(blk + 2 * d, n_blk)
            out.append(send(mine, mine, x_send.at[layer, h, d], x_recv.at[layer, h, d], "blk", to))
        near = send(mine, mine, x_send.at[layer, h, 0], x_recv.at[layer, h, 0], "blk", mate)
        return out, near

    def pass_on(layer, h, arriving):
        out, near = arriving
        passed = [near]
        for d in range(1, n_chip):
            out[d - 1].wait_recv()
            source = lax.rem(blk + n_blk - 2 * d, n_blk)
            theirs = x_in.at[layer, source, span(h)]
            at = n_chip + d - 1
            passed.append(
                send(theirs, theirs, x_send.at[layer, h, at], x_recv.at[layer, h, at], "blk", mate)
            )
        return passed

    arriving = [share_out(0, h) for h in range(HALVES)]

    unit_row = lax.broadcasted_iota(jnp.int32, (edge, edge), 0)
    unit_col = lax.broadcasted_iota(jnp.int32, (edge, edge), 1)
    unit = jnp.where(unit_row == unit_col, 1.0, 0.0).astype(BF16)
    for load in loads[1:4]:
        load.wait()

    def densify(first, last):
        @pl.loop(first, last)
        def _(r):
            lanes = pl.ds(pl.multiple_of(r * edge, edge), edge)
            for s in range(n_blk):
                count = tile_count[r, s]
                named = [
                    jnp.where(k < count, col_local[r, s * slot_count + k], -1)
                    for k in range(slot_count)
                ]
                for c in range(row_blocks):
                    slot = jnp.int32(-1)
                    for k in range(slot_count):
                        slot = jnp.where(named[k] == c, s * slot_count + k, slot)
                    tile = tiles[r, jnp.maximum(slot, 0)].astype(dense.dtype)
                    dense[s * row_blocks + c, :, lanes] = jnp.where(
                        slot >= 0, tile, jnp.zeros_like(tile)
                    )
            turned = contract(unit, flat(dense[:, :, lanes]), 1, 1).astype(dense_t.dtype)
            for q in range(n_rep):
                dense_t[q, r] = turned[q * share : (q + 1) * share]

    densify(0, half_blocks)
    arriving = [pass_on(0, h, arriving[h]) for h in range(HALVES)]
    densify(half_blocks, row_blocks)
    for load in loads[4:]:
        load.wait()

    def aggregate(layer, arriving):
        for passed in arriving:
            for copy in passed:
                copy.wait_recv()
        x = x_in[layer].reshape(n_blk * rows, width)
        copies = []
        for h in range(HALVES):
            at = pl.ds(h * half_blocks, half_blocks)
            of_half = []
            for d in range(1, n_rep):
                part = jnp.dot(flat(dense_t[rep_to[d], at]), x, preferred_element_type=F32)
                agg_out[layer, d - 1, span(h)] = part.astype(BF16)
                of_half.append(
                    send(
                        agg_out.at[layer, d - 1, span(h)],
                        agg_in.at[layer, d - 1, span(h)],
                        agg_send.at[layer, h, d],
                        agg_recv.at[layer, h, d],
                        "rep",
                        rep_to[d],
                    )
                )
            copies.append(of_half)
        agg_keep[...] = jnp.dot(flat(dense_t[rep]), x, preferred_element_type=F32)
        return copies

    def finish_aggregate(layer, h, copies):
        total = agg_keep[span(h)]
        for d, copy in enumerate(copies[h]):
            copy.wait_recv()
            total = total + agg_in[layer, d, span(h)].astype(F32)
        return total.astype(BF16)

    summing = aggregate(0, arriving)

    cot_share = flat(cot[:, rep])
    back = contract(flat(cot[...].reshape(row_blocks * n_rep, share, width)), w_neigh[1], 1, 1).astype(BF16)
    spreading = []
    for d in range(1, n_blk):
        to = dense[pl.ds(blk_to[d] * row_blocks, row_blocks)]
        spread_out[d - 1] = jnp.dot(flat(to), back, preferred_element_type=F32).astype(BF16)
        spreading.append(
            send(
                spread_out.at[d - 1],
                spread_in.at[d - 1],
                spread_send.at[d],
                spread_recv.at[d],
                "blk",
                blk_to[d],
            )
        )
    own = dense[pl.ds(blk * row_blocks, row_blocks)]
    hidden_grad = jnp.dot(flat(own), back, preferred_element_type=F32) + contract(
        cot_share, w_self[1], 1, 1
    )

    z0_part = jnp.dot(feats_share, w_self[0], preferred_element_type=F32) + bias[0:1]
    agg0, z0, sigma, arriving = [], [], [], []
    for h in range(HALVES):
        at = slice(h * half_rows, (h + 1) * half_rows)
        agg0.append(finish_aggregate(0, h, summing))
        z0.append(z0_part[at] + jnp.dot(agg0[h], w_neigh[0], preferred_element_type=F32))
        sigma.append(1.0 / (1.0 + jnp.exp(-z0[h])))
        x_in[1, blk, span(h)] = (z0[h] * sigma[h]).astype(BF16)
        arriving.append(share_out(1, h))
    agg0 = jnp.concatenate(agg0, axis=0)
    z0 = jnp.concatenate(z0, axis=0)
    sigma = jnp.concatenate(sigma, axis=0)
    h1 = x_in[1, blk]
    arriving[0] = pass_on(1, 0, arriving[0])

    for d, copy in enumerate(spreading):
        copy.wait_recv()
        hidden_grad = hidden_grad + spread_in[d].astype(F32)
    dh1 = hidden_grad.astype(BF16).astype(F32)
    dz0 = (dh1 * sigma * (1.0 + z0 * (1.0 - sigma))).astype(BF16)
    for h in range(1, HALVES):
        arriving[h] = pass_on(1, h, arriving[h])

    summing = aggregate(1, arriving)

    def place(at, value):
        for q in range(n_blk):
            part[q, at * piece : (at + 1) * piece] = value[q * piece : (q + 1) * piece]

    place(0, contract(feats_share, dz0, 0, 0))
    place(1, contract(agg0, dz0, 0, 0))
    place(2, contract(h1, cot_share, 0, 0))
    neigh_one = contract(agg_keep[...].astype(BF16), cot_share, 0, 0)
    for d in range(1, n_rep):
        neigh_one = neigh_one + contract(agg_out[1, d - 1], flat(cot[:, rep_to[d]]), 0, 0)
    place(3, neigh_one)
    bias_rows = jnp.concatenate(
        [
            jnp.sum(dz0.astype(F32), axis=0, keepdims=True),
            jnp.sum(cot_share.astype(F32), axis=0, keepdims=True),
            jnp.zeros((14, width), F32),
        ],
        axis=0,
    )
    for q in range(n_blk):
        part[q, 4 * piece :] = bias_rows
    scattering = [
        send(
            part.at[blk_to[d]],
            blk_in.at[d - 1],
            grad_send.at[0, d],
            grad_recv.at[0, d],
            "blk",
            blk_to[d],
        )
        for d in range(1, n_blk)
    ]
    z1_part = jnp.dot(h1, w_self[1], preferred_element_type=F32) + bias[1:2]

    total = part[blk]
    for d, copy in enumerate(scattering):
        copy.wait_recv()
        total = total + blk_in[d]
    half[...] = total.astype(BF16)
    swapping = [
        send(
            half,
            rep_in.at[d - 1],
            grad_send.at[1, d],
            grad_recv.at[1, d],
            "rep",
            rep_to[d],
        )
        for d in range(1, n_rep)
    ]

    gathering = []
    for h in range(HALVES):
        at = slice(h * half_rows, (h + 1) * half_rows)
        agg1 = finish_aggregate(1, h, summing)
        z1 = z1_part[at] + jnp.dot(agg1, w_neigh[1], preferred_element_type=F32)
        logits_in[rep, span(h)] = z1.astype(BF16)
        gathering += [
            send(
                logits_in.at[rep, span(h)],
                logits_in.at[rep, span(h)],
                logits_send.at[h, d],
                logits_recv.at[h, d],
                "rep",
                rep_to[d],
            )
            for d in range(1, n_rep)
        ]

    for copy in swapping:
        copy.wait_recv()
    rep_in[n_rep - 1] = half[...]

    def of(q):
        return rep_in[lax.rem(rep + 2 * n_rep - 1 - q, n_rep)].astype(F32)

    total = of(0)
    for q in range(1, n_rep):
        total = total + of(q)
    full[blk] = total
    spreading_out = [
        send(
            full.at[blk],
            full.at[blk],
            grad_send.at[2, d],
            grad_recv.at[2, d],
            "blk",
            blk_to[d],
        )
        for d in range(1, n_blk)
    ]
    for copy in spreading_out:
        copy.wait_recv()
    for q in range(n_blk):
        at = slice(q * piece, (q + 1) * piece)
        grad_self[0, at] = full[q, 0:piece]
        grad_neigh[0, at] = full[q, piece : 2 * piece]
        grad_self[1, at] = full[q, 2 * piece : 3 * piece]
        grad_neigh[1, at] = full[q, 3 * piece : 4 * piece]
    grad_bias[...] = full[0, 4 * piece : 4 * piece + 2]

    for copy in gathering:
        copy.wait_recv()
    for q in range(n_rep):
        logits[:, q] = blocks_of(logits_in[q])
    for copy in sends:
        copy.wait_send()


def solution(mesh):
    n_blk, n_rep = mesh.shape["blk"], mesh.shape["rep"]

    def shards(feats, tiles, col_local, tile_count, w_self, w_neigh, bias, cotangent):
        row_blocks, slots, share, edge = tiles.shape
        width = feats.shape[1]
        rows = row_blocks * share
        piece = width // n_blk
        held = BF16 if share % 16 == 0 else F32
        vmem = pl.BlockSpec(memory_space=pltpu.VMEM)
        split = (row_blocks, n_rep, share, width)
        dma = pltpu.SemaphoreType.DMA
        grad_rows = 4 * piece + 16
        wide = max(n_blk, n_rep)
        anywhere = pl.BlockSpec(memory_space=pl.ANY)
        logits, grad_self, grad_neigh, grad_bias = pl.pallas_call(
            functools.partial(kernel, n_blk, n_rep),
            out_shape=(
                jax.ShapeDtypeStruct(split, BF16),
                jax.ShapeDtypeStruct((2, width, width), F32),
                jax.ShapeDtypeStruct((2, width, width), F32),
                jax.ShapeDtypeStruct((2, width), F32),
            ),
            in_specs=[anywhere] * 8,
            out_specs=(vmem, vmem, vmem, vmem),
            scratch_shapes=[
                pltpu.VMEM(split, BF16),
                pltpu.VMEM(tiles.shape, BF16),
                pltpu.SMEM(col_local.shape, jnp.int32),
                pltpu.SMEM(tile_count.shape, jnp.int32),
                pltpu.VMEM(w_self.shape, BF16),
                pltpu.VMEM(w_neigh.shape, BF16),
                pltpu.VMEM(bias.shape, F32),
                pltpu.VMEM(split, BF16),
                pltpu.VMEM((n_blk * row_blocks, share, row_blocks * edge), held),
                pltpu.VMEM((n_rep, row_blocks, share, n_blk * rows), held),
                pltpu.VMEM((rows, width), F32),
                pltpu.VMEM((2, n_blk, rows, width), BF16),
                pltpu.VMEM((n_blk - 1, rows, width), BF16),
                pltpu.VMEM((n_blk - 1, rows, width), BF16),
                pltpu.VMEM((2, n_rep - 1, rows, width), BF16),
                pltpu.VMEM((2, n_rep - 1, rows, width), BF16),
                pltpu.VMEM((n_rep, rows, width), BF16),
                pltpu.VMEM((n_blk, grad_rows, width), F32),
                pltpu.VMEM((n_blk - 1, grad_rows, width), F32),
                pltpu.VMEM((grad_rows, width), BF16),
                pltpu.VMEM((n_rep, grad_rows, width), BF16),
                pltpu.VMEM((n_blk, grad_rows, width), F32),
                dma((8,)),
                dma((2, HALVES, n_blk)),
                dma((2, HALVES, n_blk)),
                dma((n_blk,)),
                dma((n_blk,)),
                dma((2, HALVES, n_rep)),
                dma((2, HALVES, n_rep)),
                dma((HALVES, n_rep)),
                dma((HALVES, n_rep)),
                dma((3, wide)),
                dma((3, wide)),
            ],
            compiler_params=pltpu.CompilerParams(
                collective_id=0, has_side_effects=True, vmem_limit_bytes=52 * 2**20
            ),
        )(
            feats.reshape(split),
            tiles,
            col_local,
            tile_count,
            w_self,
            w_neigh,
            bias,
            cotangent.reshape(split),
        )
        return logits.reshape(feats.shape), grad_self, grad_neigh, grad_bias

    return jax.shard_map(
        shards,
        mesh=mesh,
        in_specs=(
            P(("group", "blk"), None),
            P(("group", "blk"), None, "rep", None),
            P(("group", "blk"), None),
            P(("group", "blk"), None),
            P(),
            P(),
            P(),
            P(("group", "blk"), None),
        ),
        out_specs=(
            P(("group", "blk"), None),
            P("group", None, None),
            P("group", None, None),
            P("group", None),
        ),
        check_vma=False,
    )
```

```python
import functools

import jax
import jax.numpy as jnp
from jax import lax
from jax.experimental import pallas as pl
from jax.experimental.pallas import tpu as pltpu
from jax.sharding import PartitionSpec as P

MESH = pl.DeviceIdType.MESH
F32 = jnp.float32
BF16 = jnp.bfloat16
HALVES = 2


def contract(a, b, a_dim, b_dim):
    return lax.dot_general(a, b, (((a_dim,), (b_dim,)), ((), ())), preferred_element_type=F32)


def kernel(
    n_blk,
    n_rep,
    feats_hbm,
    tiles_hbm,
    col_hbm,
    count_hbm,
    w_self_hbm,
    w_neigh_hbm,
    bias_hbm,
    cot_hbm,
    logits,
    grad_self,
    grad_neigh,
    grad_bias,
    feats,
    tiles,
    col_local,
    tile_count,
    w_self,
    w_neigh,
    bias,
    cot,
    dense,
    dense_t,
    agg_keep,
    x_in,
    spread_out,
    spread_in,
    agg_out,
    agg_in,
    logits_in,
    part,
    blk_in,
    half,
    rep_in,
    full,
    load_sem,
    x_send,
    x_recv,
    spread_send,
    spread_recv,
    agg_send,
    agg_recv,
    logits_send,
    logits_recv,
    grad_send,
    grad_recv,
):
    row_blocks, slots, share, edge = tiles.shape
    slot_count = slots // n_blk
    width = feats.shape[-1]
    rows = row_blocks * share
    piece = width // n_blk
    n_chip = n_blk // 2
    half_blocks = row_blocks // HALVES
    half_rows = rows // HALVES
    blk = lax.axis_index("blk")
    rep = lax.axis_index("rep")
    whole_tiles = share % 16 == 0

    def flat(value):
        if whole_tiles:
            return value.reshape(-1, value.shape[-1]).astype(BF16)
        return value.astype(F32).reshape(-1, value.shape[-1]).astype(BF16)

    def blocks_of(value):
        if whole_tiles:
            return value.reshape(row_blocks, share, width)
        return value.astype(F32).reshape(row_blocks, share, width).astype(BF16)

    sends = []

    def send(source, target, send_sem, recv_sem, axis, partner):
        copy = pltpu.make_async_remote_copy(
            src_ref=source,
            dst_ref=target,
            send_sem=send_sem,
            recv_sem=recv_sem,
            device_id={axis: partner},
            device_id_type=MESH,
        )
        copy.start()
        sends.append(copy)
        return copy

    blk_to = [lax.rem(blk + d, n_blk) for d in range(n_blk)]
    rep_to = [lax.rem(rep + d, n_rep) for d in range(n_rep)]
    core = lax.rem(blk, 2)
    mate = blk + 1 - 2 * core

    barrier = pltpu.get_barrier_semaphore()
    for d in range(1, n_blk):
        pl.semaphore_signal(barrier, inc=1, device_id={"blk": blk_to[d]}, device_id_type=MESH)
    for d in range(1, n_rep):
        pl.semaphore_signal(barrier, inc=1, device_id={"rep": rep_to[d]}, device_id_type=MESH)

    pairs = [
        (feats_hbm, feats),
        (col_hbm, col_local),
        (count_hbm, tile_count),
        (tiles_hbm, tiles),
        (cot_hbm, cot),
        (w_self_hbm, w_self),
        (w_neigh_hbm, w_neigh),
        (bias_hbm, bias),
    ]
    loads = [pltpu.make_async_copy(a, b, load_sem.at[i]) for i, (a, b) in enumerate(pairs)]
    for load in loads:
        load.start()
    loads[0].wait()
    feats_share = flat(feats[:, rep])
    x_in[0, blk] = feats_share
    pl.semaphore_wait(barrier, n_blk - 1 + n_rep - 1)

    def span(h):
        return pl.ds(h * half_rows, half_rows)

    def share_out(layer, h):
        mine = x_in.at[layer, blk, span(h)]
        out = []
        for d in range(1, n_chip):
            to = lax.rem(blk + 2 * d, n_blk)
            out.append(send(mine, mine, x_send.at[layer, h, d], x_recv.at[layer, h, d], "blk", to))
        near = send(mine, mine, x_send.at[layer, h, 0], x_recv.at[layer, h, 0], "blk", mate)
        return out, near

    def pass_on(layer, h, arriving):
        out, near = arriving
        passed = [near]
        for d in range(1, n_chip):
            out[d - 1].wait_recv()
            source = lax.rem(blk + n_blk - 2 * d, n_blk)
            theirs = x_in.at[layer, source, span(h)]
            at = n_chip + d - 1
            passed.append(
                send(theirs, theirs, x_send.at[layer, h, at], x_recv.at[layer, h, at], "blk", mate)
            )
        return passed

    arriving = [share_out(0, h) for h in range(HALVES)]

    unit_row = lax.broadcasted_iota(jnp.int32, (edge, edge), 0)
    unit_col = lax.broadcasted_iota(jnp.int32, (edge, edge), 1)
    unit = jnp.where(unit_row == unit_col, 1.0, 0.0).astype(BF16)
    for load in loads[1:4]:
        load.wait()

    def densify(first, last):
        @pl.loop(first, last)
        def _(r):
            lanes = pl.ds(pl.multiple_of(r * edge, edge), edge)
            for s in range(n_blk):
                count = tile_count[s, r]
                named = [
                    jnp.where(k < count, col_local[r, s * slot_count + k], -1)
                    for k in range(slot_count)
                ]
                for c in range(row_blocks):
                    slot = jnp.int32(-1)
                    for k in range(slot_count):
                        slot = jnp.where(named[k] == c, s * slot_count + k, slot)
                    tile = tiles[r, jnp.maximum(slot, 0)].astype(dense.dtype)
                    dense[s * row_blocks + c, :, lanes] = jnp.where(
                        slot >= 0, tile, jnp.zeros_like(tile)
                    )
            turned = contract(unit, flat(dense[:, :, lanes]), 1, 1).astype(dense_t.dtype)
            for q in range(n_rep):
                dense_t[q, r] = turned[q * share : (q + 1) * share]

    densify(0, half_blocks)
    arriving = [pass_on(0, h, arriving[h]) for h in range(HALVES)]
    densify(half_blocks, row_blocks)
    for load in loads[4:]:
        load.wait()

    def aggregate(layer, arriving):
        for passed in arriving:
            for copy in passed:
                copy.wait_recv()
        x = x_in[layer].reshape(n_blk * rows, width)
        copies = []
        for h in range(HALVES):
            at = pl.ds(h * half_blocks, half_blocks)
            of_half = []
            for d in range(1, n_rep):
                part = jnp.dot(flat(dense_t[rep_to[d], at]), x, preferred_element_type=F32)
                agg_out[layer, d - 1, span(h)] = part.astype(BF16)
                of_half.append(
                    send(
                        agg_out.at[layer, d - 1, span(h)],
                        agg_in.at[layer, d - 1, span(h)],
                        agg_send.at[layer, h, d],
                        agg_recv.at[layer, h, d],
                        "rep",
                        rep_to[d],
                    )
                )
            copies.append(of_half)
        agg_keep[...] = jnp.dot(flat(dense_t[rep]), x, preferred_element_type=F32)
        return copies

    def finish_aggregate(layer, h, copies):
        total = agg_keep[span(h)]
        for d, copy in enumerate(copies[h]):
            copy.wait_recv()
            total = total + agg_in[layer, d, span(h)].astype(F32)
        return total.astype(BF16)

    summing = aggregate(0, arriving)

    cot_share = flat(cot[:, rep])
    back = contract(flat(cot[...].reshape(row_blocks * n_rep, share, width)), w_neigh[1], 1, 1).astype(BF16)
    spreading = []
    for d in range(1, n_blk):
        to = dense[pl.ds(blk_to[d] * row_blocks, row_blocks)]
        spread_out[d - 1] = jnp.dot(flat(to), back, preferred_element_type=F32).astype(BF16)
        spreading.append(
            send(
                spread_out.at[d - 1],
                spread_in.at[d - 1],
                spread_send.at[d],
                spread_recv.at[d],
                "blk",
                blk_to[d],
            )
        )
    own = dense[pl.ds(blk * row_blocks, row_blocks)]
    hidden_grad = jnp.dot(flat(own), back, preferred_element_type=F32) + contract(
        cot_share, w_self[1], 1, 1
    )

    z0_part = jnp.dot(feats_share, w_self[0], preferred_element_type=F32) + bias[0:1]
    agg0, z0, sigma, arriving = [], [], [], []
    for h in range(HALVES):
        at = slice(h * half_rows, (h + 1) * half_rows)
        agg0.append(finish_aggregate(0, h, summing))
        z0.append(z0_part[at] + jnp.dot(agg0[h], w_neigh[0], preferred_element_type=F32))
        sigma.append(1.0 / (1.0 + jnp.exp(-z0[h])))
        x_in[1, blk, span(h)] = (z0[h] * sigma[h]).astype(BF16)
        arriving.append(share_out(1, h))
    agg0 = jnp.concatenate(agg0, axis=0)
    z0 = jnp.concatenate(z0, axis=0)
    sigma = jnp.concatenate(sigma, axis=0)
    h1 = x_in[1, blk]
    arriving[0] = pass_on(1, 0, arriving[0])

    for d, copy in enumerate(spreading):
        copy.wait_recv()
        hidden_grad = hidden_grad + spread_in[d].astype(F32)
    dh1 = hidden_grad.astype(BF16).astype(F32)
    dz0 = (dh1 * sigma * (1.0 + z0 * (1.0 - sigma))).astype(BF16)
    for h in range(1, HALVES):
        arriving[h] = pass_on(1, h, arriving[h])

    summing = aggregate(1, arriving)

    def place(at, value):
        for q in range(n_blk):
            part[q, at * piece : (at + 1) * piece] = value[q * piece : (q + 1) * piece]

    place(0, contract(feats_share, dz0, 0, 0))
    place(1, contract(agg0, dz0, 0, 0))
    place(2, contract(h1, cot_share, 0, 0))
    neigh_one = contract(agg_keep[...].astype(BF16), cot_share, 0, 0)
    for d in range(1, n_rep):
        neigh_one = neigh_one + contract(agg_out[1, d - 1], flat(cot[:, rep_to[d]]), 0, 0)
    place(3, neigh_one)
    bias_rows = jnp.concatenate(
        [
            jnp.sum(dz0.astype(F32), axis=0, keepdims=True),
            jnp.sum(cot_share.astype(F32), axis=0, keepdims=True),
            jnp.zeros((14, width), F32),
        ],
        axis=0,
    )
    for q in range(n_blk):
        part[q, 4 * piece :] = bias_rows
    scattering = [
        send(
            part.at[blk_to[d]],
            blk_in.at[d - 1],
            grad_send.at[0, d],
            grad_recv.at[0, d],
            "blk",
            blk_to[d],
        )
        for d in range(1, n_blk)
    ]
    z1_part = jnp.dot(h1, w_self[1], preferred_element_type=F32) + bias[1:2]

    total = part[blk]
    for d, copy in enumerate(scattering):
        copy.wait_recv()
        total = total + blk_in[d]
    half[...] = total.astype(BF16)
    swapping = [
        send(
            half,
            rep_in.at[d - 1],
            grad_send.at[1, d],
            grad_recv.at[1, d],
            "rep",
            rep_to[d],
        )
        for d in range(1, n_rep)
    ]

    gathering = []
    for h in range(HALVES):
        at = slice(h * half_rows, (h + 1) * half_rows)
        agg1 = finish_aggregate(1, h, summing)
        z1 = z1_part[at] + jnp.dot(agg1, w_neigh[1], preferred_element_type=F32)
        logits_in[rep, span(h)] = z1.astype(BF16)
        gathering += [
            send(
                logits_in.at[rep, span(h)],
                logits_in.at[rep, span(h)],
                logits_send.at[h, d],
                logits_recv.at[h, d],
                "rep",
                rep_to[d],
            )
            for d in range(1, n_rep)
        ]

    for copy in swapping:
        copy.wait_recv()
    rep_in[n_rep - 1] = half[...]

    def of(q):
        return rep_in[lax.rem(rep + 2 * n_rep - 1 - q, n_rep)].astype(F32)

    total = of(0)
    for q in range(1, n_rep):
        total = total + of(q)
    full[blk] = total
    spreading_out = [
        send(
            full.at[blk],
            full.at[blk],
            grad_send.at[2, d],
            grad_recv.at[2, d],
            "blk",
            blk_to[d],
        )
        for d in range(1, n_blk)
    ]
    for copy in spreading_out:
        copy.wait_recv()
    for q in range(n_blk):
        at = slice(q * piece, (q + 1) * piece)
        grad_self[0, at] = full[q, 0:piece]
        grad_neigh[0, at] = full[q, piece : 2 * piece]
        grad_self[1, at] = full[q, 2 * piece : 3 * piece]
        grad_neigh[1, at] = full[q, 3 * piece : 4 * piece]
    grad_bias[...] = full[0, 4 * piece : 4 * piece + 2]

    for copy in gathering:
        copy.wait_recv()
    for q in range(n_rep):
        logits[:, q] = blocks_of(logits_in[q])
    for copy in sends:
        copy.wait_send()


def solution(mesh):
    n_blk, n_rep = mesh.shape["blk"], mesh.shape["rep"]

    def shards(feats, tiles, col_local, tile_count, w_self, w_neigh, bias, cotangent):
        row_blocks, slots, share, edge = tiles.shape
        width = feats.shape[1]
        rows = row_blocks * share
        piece = width // n_blk
        held = BF16 if share % 16 == 0 else F32
        vmem = pl.BlockSpec(memory_space=pltpu.VMEM)
        split = (row_blocks, n_rep, share, width)
        dma = pltpu.SemaphoreType.DMA
        grad_rows = 4 * piece + 16
        wide = max(n_blk, n_rep)
        anywhere = pl.BlockSpec(memory_space=pl.ANY)
        made = pl.pallas_call(
            functools.partial(kernel, n_blk, n_rep),
            out_shape=(
                jax.ShapeDtypeStruct(split, BF16),
                jax.ShapeDtypeStruct((2, width, width), F32),
                jax.ShapeDtypeStruct((2, width, width), F32),
                jax.ShapeDtypeStruct((2, width), F32),
            ),
            in_specs=[anywhere] * 8,
            out_specs=(vmem, vmem, vmem, vmem),
            scratch_shapes=[
                pltpu.VMEM(split, BF16),
                pltpu.VMEM(tiles.shape, BF16),
                pltpu.SMEM(col_local.shape, jnp.int32),
                pltpu.SMEM(tile_count.shape[::-1], jnp.int32),
                pltpu.VMEM(w_self.shape, BF16),
                pltpu.VMEM(w_neigh.shape, BF16),
                pltpu.VMEM(bias.shape, F32),
                pltpu.VMEM(split, BF16),
                pltpu.VMEM((n_blk * row_blocks, share, row_blocks * edge), held),
                pltpu.VMEM((n_rep, row_blocks, share, n_blk * rows), held),
                pltpu.VMEM((rows, width), F32),
                pltpu.VMEM((2, n_blk, rows, width), BF16),
                pltpu.VMEM((n_blk - 1, rows, width), BF16),
                pltpu.VMEM((n_blk - 1, rows, width), BF16),
                pltpu.VMEM((2, n_rep - 1, rows, width), BF16),
                pltpu.VMEM((2, n_rep - 1, rows, width), BF16),
                pltpu.VMEM((n_rep, rows, width), BF16),
                pltpu.VMEM((n_blk, grad_rows, width), F32),
                pltpu.VMEM((n_blk - 1, grad_rows, width), F32),
                pltpu.VMEM((grad_rows, width), BF16),
                pltpu.VMEM((n_rep, grad_rows, width), BF16),
                pltpu.VMEM((n_blk, grad_rows, width), F32),
                dma((8,)),
                dma((2, HALVES, n_blk)),
                dma((2, HALVES, n_blk)),
                dma((n_blk,)),
                dma((n_blk,)),
                dma((2, HALVES, n_rep)),
                dma((2, HALVES, n_rep)),
                dma((HALVES, n_rep)),
                dma((HALVES, n_rep)),
                dma((3, wide)),
                dma((3, wide)),
            ],
            compiler_params=pltpu.CompilerParams(
                collective_id=0, has_side_effects=True, vmem_limit_bytes=64 * 2**20 - 1400 * 2**10
            ),
        )(
            feats.reshape(split),
            tiles,
            col_local,
            tile_count.T,
            w_self,
            w_neigh,
            bias,
            cotangent.reshape(split),
        )
        logits, grad_self, grad_neigh, grad_bias = made
        return logits.reshape(feats.shape), grad_self, grad_neigh, grad_bias

    return jax.shard_map(
        shards,
        mesh=mesh,
        in_specs=(
            P(("group", "blk"), None),
            P(("group", "blk"), None, "rep", None),
            P(("group", "blk"), None),
            P(("group", "blk"), None),
            P(),
            P(),
            P(),
            P(("group", "blk"), None),
        ),
        out_specs=(
            P(("group", "blk"), None),
            P("group", None, None),
            P("group", None, None),
            P("group", None),
        ),
        check_vma=False,
    )
```

```python
import functools

import jax
import jax.numpy as jnp
from jax import lax
from jax.experimental import pallas as pl
from jax.experimental.pallas import tpu as pltpu
from jax.sharding import PartitionSpec as P

MESH = pl.DeviceIdType.MESH
F32 = jnp.float32
BF16 = jnp.bfloat16
HALVES = 3


def contract(a, b, a_dim, b_dim):
    return lax.dot_general(a, b, (((a_dim,), (b_dim,)), ((), ())), preferred_element_type=F32)


def kernel(
    n_blk,
    n_rep,
    feats_hbm,
    tiles_hbm,
    col_hbm,
    count_hbm,
    w_self_hbm,
    w_neigh_hbm,
    bias_hbm,
    cot_hbm,
    logits,
    grad_self,
    grad_neigh,
    grad_bias,
    feats,
    tiles,
    col_local,
    tile_count,
    w_self,
    w_neigh,
    bias,
    cot,
    dense,
    dense_t,
    agg_keep,
    x_in,
    spread_out,
    spread_in,
    agg_out,
    agg_in,
    logits_in,
    part,
    blk_in,
    half,
    rep_in,
    full,
    load_sem,
    x_send,
    x_recv,
    spread_send,
    spread_recv,
    agg_send,
    agg_recv,
    logits_send,
    logits_recv,
    grad_send,
    grad_recv,
):
    row_blocks, slots, share, edge = tiles.shape
    slot_count = slots // n_blk
    width = feats.shape[-1]
    rows = row_blocks * share
    piece = width // n_blk
    n_chip = n_blk // 2
    half_blocks = row_blocks // HALVES
    half_rows = rows // HALVES
    blk = lax.axis_index("blk")
    rep = lax.axis_index("rep")
    whole_tiles = share % 16 == 0

    def flat(value):
        if whole_tiles:
            return value.reshape(-1, value.shape[-1]).astype(BF16)
        return value.astype(F32).reshape(-1, value.shape[-1]).astype(BF16)

    def blocks_of(value):
        if whole_tiles:
            return value.reshape(row_blocks, share, width)
        return value.astype(F32).reshape(row_blocks, share, width).astype(BF16)

    sends = []

    def send(source, target, send_sem, recv_sem, axis, partner):
        copy = pltpu.make_async_remote_copy(
            src_ref=source,
            dst_ref=target,
            send_sem=send_sem,
            recv_sem=recv_sem,
            device_id={axis: partner},
            device_id_type=MESH,
        )
        copy.start()
        sends.append(copy)
        return copy

    blk_to = [lax.rem(blk + d, n_blk) for d in range(n_blk)]
    rep_to = [lax.rem(rep + d, n_rep) for d in range(n_rep)]
    core = lax.rem(blk, 2)
    mate = blk + 1 - 2 * core

    barrier = pltpu.get_barrier_semaphore()
    for d in range(1, n_blk):
        pl.semaphore_signal(barrier, inc=1, device_id={"blk": blk_to[d]}, device_id_type=MESH)
    for d in range(1, n_rep):
        pl.semaphore_signal(barrier, inc=1, device_id={"rep": rep_to[d]}, device_id_type=MESH)

    pairs = [
        (feats_hbm, feats),
        (col_hbm, col_local),
        (count_hbm, tile_count),
        (tiles_hbm, tiles),
        (cot_hbm, cot),
        (w_self_hbm, w_self),
        (w_neigh_hbm, w_neigh),
        (bias_hbm, bias),
    ]
    loads = [pltpu.make_async_copy(a, b, load_sem.at[i]) for i, (a, b) in enumerate(pairs)]
    for load in loads:
        load.start()
    loads[0].wait()
    feats_share = flat(feats[:, rep])
    x_in[0, blk] = feats_share
    pl.semaphore_wait(barrier, n_blk - 1 + n_rep - 1)

    def span(h):
        return pl.ds(h * half_rows, half_rows)

    def share_out(layer, h):
        mine = x_in.at[layer, blk, span(h)]
        out = []
        for d in range(1, n_chip):
            to = lax.rem(blk + 2 * d, n_blk)
            out.append(send(mine, mine, x_send.at[layer, h, d], x_recv.at[layer, h, d], "blk", to))
        near = send(mine, mine, x_send.at[layer, h, 0], x_recv.at[layer, h, 0], "blk", mate)
        return out, near

    def pass_on(layer, h, arriving):
        out, near = arriving
        passed = [near]
        for d in range(1, n_chip):
            out[d - 1].wait_recv()
            source = lax.rem(blk + n_blk - 2 * d, n_blk)
            theirs = x_in.at[layer, source, span(h)]
            at = n_chip + d - 1
            passed.append(
                send(theirs, theirs, x_send.at[layer, h, at], x_recv.at[layer, h, at], "blk", mate)
            )
        return passed

    arriving = [share_out(0, h) for h in range(HALVES)]

    unit_row = lax.broadcasted_iota(jnp.int32, (edge, edge), 0)
    unit_col = lax.broadcasted_iota(jnp.int32, (edge, edge), 1)
    unit = jnp.where(unit_row == unit_col, 1.0, 0.0).astype(BF16)
    for load in loads[1:4]:
        load.wait()

    def densify(first, last):
        @pl.loop(first, last)
        def _(r):
            lanes = pl.ds(pl.multiple_of(r * edge, edge), edge)
            for s in range(n_blk):
                count = tile_count[s, r]
                named = [
                    jnp.where(k < count, col_local[r, s * slot_count + k], -1)
                    for k in range(slot_count)
                ]
                for c in range(row_blocks):
                    slot = jnp.int32(-1)
                    for k in range(slot_count):
                        slot = jnp.where(named[k] == c, s * slot_count + k, slot)
                    tile = tiles[r, jnp.maximum(slot, 0)].astype(dense.dtype)
                    dense[s * row_blocks + c, :, lanes] = jnp.where(
                        slot >= 0, tile, jnp.zeros_like(tile)
                    )
            turned = contract(unit, flat(dense[:, :, lanes]), 1, 1).astype(dense_t.dtype)
            for q in range(n_rep):
                dense_t[q, r] = turned[q * share : (q + 1) * share]

    densify(0, half_blocks)
    arriving = [pass_on(0, h, arriving[h]) for h in range(HALVES)]
    densify(half_blocks, row_blocks)
    for load in loads[4:]:
        load.wait()

    def aggregate(layer, arriving):
        for passed in arriving:
            for copy in passed:
                copy.wait_recv()
        x = x_in[layer].reshape(n_blk * rows, width)
        copies = []
        for h in range(HALVES):
            at = pl.ds(h * half_blocks, half_blocks)
            of_half = []
            for d in range(1, n_rep):
                part = jnp.dot(flat(dense_t[rep_to[d], at]), x, preferred_element_type=F32)
                agg_out[layer, d - 1, span(h)] = part.astype(BF16)
                of_half.append(
                    send(
                        agg_out.at[layer, d - 1, span(h)],
                        agg_in.at[layer, d - 1, span(h)],
                        agg_send.at[layer, h, d],
                        agg_recv.at[layer, h, d],
                        "rep",
                        rep_to[d],
                    )
                )
            copies.append(of_half)
        agg_keep[...] = jnp.dot(flat(dense_t[rep]), x, preferred_element_type=F32)
        return copies

    def finish_aggregate(layer, h, copies):
        total = agg_keep[span(h)]
        for d, copy in enumerate(copies[h]):
            copy.wait_recv()
            total = total + agg_in[layer, d, span(h)].astype(F32)
        return total.astype(BF16)

    summing = aggregate(0, arriving)

    cot_share = flat(cot[:, rep])
    back = contract(flat(cot[...].reshape(row_blocks * n_rep, share, width)), w_neigh[1], 1, 1).astype(BF16)
    spreading = []
    for d in range(1, n_blk):
        to = dense[pl.ds(blk_to[d] * row_blocks, row_blocks)]
        spread_out[d - 1] = jnp.dot(flat(to), back, preferred_element_type=F32).astype(BF16)
        spreading.append(
            send(
                spread_out.at[d - 1],
                spread_in.at[d - 1],
                spread_send.at[d],
                spread_recv.at[d],
                "blk",
                blk_to[d],
            )
        )
    own = dense[pl.ds(blk * row_blocks, row_blocks)]
    hidden_grad = jnp.dot(flat(own), back, preferred_element_type=F32) + contract(
        cot_share, w_self[1], 1, 1
    )

    z0_part = jnp.dot(feats_share, w_self[0], preferred_element_type=F32) + bias[0:1]
    agg0, z0, sigma, arriving = [], [], [], []
    for h in range(HALVES):
        at = slice(h * half_rows, (h + 1) * half_rows)
        agg0.append(finish_aggregate(0, h, summing))
        z0.append(z0_part[at] + jnp.dot(agg0[h], w_neigh[0], preferred_element_type=F32))
        sigma.append(1.0 / (1.0 + jnp.exp(-z0[h])))
        x_in[1, blk, span(h)] = (z0[h] * sigma[h]).astype(BF16)
        arriving.append(share_out(1, h))
    agg0 = jnp.concatenate(agg0, axis=0)
    z0 = jnp.concatenate(z0, axis=0)
    sigma = jnp.concatenate(sigma, axis=0)
    h1 = x_in[1, blk]
    arriving[0] = pass_on(1, 0, arriving[0])

    for d, copy in enumerate(spreading):
        copy.wait_recv()
        hidden_grad = hidden_grad + spread_in[d].astype(F32)
    dh1 = hidden_grad.astype(BF16).astype(F32)
    dz0 = (dh1 * sigma * (1.0 + z0 * (1.0 - sigma))).astype(BF16)
    for h in range(1, HALVES):
        arriving[h] = pass_on(1, h, arriving[h])

    summing = aggregate(1, arriving)

    def place(at, value):
        for q in range(n_blk):
            part[q, at * piece : (at + 1) * piece] = value[q * piece : (q + 1) * piece]

    place(0, contract(feats_share, dz0, 0, 0))
    place(1, contract(agg0, dz0, 0, 0))
    place(2, contract(h1, cot_share, 0, 0))
    neigh_one = contract(agg_keep[...].astype(BF16), cot_share, 0, 0)
    for d in range(1, n_rep):
        neigh_one = neigh_one + contract(agg_out[1, d - 1], flat(cot[:, rep_to[d]]), 0, 0)
    place(3, neigh_one)
    bias_rows = jnp.concatenate(
        [
            jnp.sum(dz0.astype(F32), axis=0, keepdims=True),
            jnp.sum(cot_share.astype(F32), axis=0, keepdims=True),
            jnp.zeros((14, width), F32),
        ],
        axis=0,
    )
    for q in range(n_blk):
        part[q, 4 * piece :] = bias_rows
    scattering = [
        send(
            part.at[blk_to[d]],
            blk_in.at[d - 1],
            grad_send.at[0, d],
            grad_recv.at[0, d],
            "blk",
            blk_to[d],
        )
        for d in range(1, n_blk)
    ]
    z1_part = jnp.dot(h1, w_self[1], preferred_element_type=F32) + bias[1:2]

    total = part[blk]
    for d, copy in enumerate(scattering):
        copy.wait_recv()
        total = total + blk_in[d]
    half[...] = total.astype(BF16)
    swapping = [
        send(
            half,
            rep_in.at[d - 1],
            grad_send.at[1, d],
            grad_recv.at[1, d],
            "rep",
            rep_to[d],
        )
        for d in range(1, n_rep)
    ]

    gathering = []
    for h in range(HALVES):
        at = slice(h * half_rows, (h + 1) * half_rows)
        agg1 = finish_aggregate(1, h, summing)
        z1 = z1_part[at] + jnp.dot(agg1, w_neigh[1], preferred_element_type=F32)
        logits_in[rep, span(h)] = z1.astype(BF16)
        gathering += [
            send(
                logits_in.at[rep, span(h)],
                logits_in.at[rep, span(h)],
                logits_send.at[h, d],
                logits_recv.at[h, d],
                "rep",
                rep_to[d],
            )
            for d in range(1, n_rep)
        ]

    for copy in swapping:
        copy.wait_recv()
    rep_in[n_rep - 1] = half[...]

    def of(q):
        return rep_in[lax.rem(rep + 2 * n_rep - 1 - q, n_rep)].astype(F32)

    total = of(0)
    for q in range(1, n_rep):
        total = total + of(q)
    full[blk] = total
    spreading_out = [
        send(
            full.at[blk],
            full.at[blk],
            grad_send.at[2, d],
            grad_recv.at[2, d],
            "blk",
            blk_to[d],
        )
        for d in range(1, n_blk)
    ]
    for copy in spreading_out:
        copy.wait_recv()
    for q in range(n_blk):
        at = slice(q * piece, (q + 1) * piece)
        grad_self[0, at] = full[q, 0:piece]
        grad_neigh[0, at] = full[q, piece : 2 * piece]
        grad_self[1, at] = full[q, 2 * piece : 3 * piece]
        grad_neigh[1, at] = full[q, 3 * piece : 4 * piece]
    grad_bias[...] = full[0, 4 * piece : 4 * piece + 2]

    for copy in gathering:
        copy.wait_recv()
    for q in range(n_rep):
        logits[:, q] = blocks_of(logits_in[q])
    for copy in sends:
        copy.wait_send()


def solution(mesh):
    n_blk, n_rep = mesh.shape["blk"], mesh.shape["rep"]

    def shards(feats, tiles, col_local, tile_count, w_self, w_neigh, bias, cotangent):
        row_blocks, slots, share, edge = tiles.shape
        width = feats.shape[1]
        rows = row_blocks * share
        piece = width // n_blk
        held = BF16 if share % 16 == 0 else F32
        vmem = pl.BlockSpec(memory_space=pltpu.VMEM)
        split = (row_blocks, n_rep, share, width)
        dma = pltpu.SemaphoreType.DMA
        grad_rows = 4 * piece + 16
        wide = max(n_blk, n_rep)
        anywhere = pl.BlockSpec(memory_space=pl.ANY)
        made = pl.pallas_call(
            functools.partial(kernel, n_blk, n_rep),
            out_shape=(
                jax.ShapeDtypeStruct(split, BF16),
                jax.ShapeDtypeStruct((2, width, width), F32),
                jax.ShapeDtypeStruct((2, width, width), F32),
                jax.ShapeDtypeStruct((2, width), F32),
            ),
            in_specs=[anywhere] * 8,
            out_specs=(vmem, vmem, vmem, vmem),
            scratch_shapes=[
                pltpu.VMEM(split, BF16),
                pltpu.VMEM(tiles.shape, BF16),
                pltpu.SMEM(col_local.shape, jnp.int32),
                pltpu.SMEM(tile_count.shape[::-1], jnp.int32),
                pltpu.VMEM(w_self.shape, BF16),
                pltpu.VMEM(w_neigh.shape, BF16),
                pltpu.VMEM(bias.shape, F32),
                pltpu.VMEM(split, BF16),
                pltpu.VMEM((n_blk * row_blocks, share, row_blocks * edge), held),
                pltpu.VMEM((n_rep, row_blocks, share, n_blk * rows), held),
                pltpu.VMEM((rows, width), F32),
                pltpu.VMEM((2, n_blk, rows, width), BF16),
                pltpu.VMEM((n_blk - 1, rows, width), BF16),
                pltpu.VMEM((n_blk - 1, rows, width), BF16),
                pltpu.VMEM((2, n_rep - 1, rows, width), BF16),
                pltpu.VMEM((2, n_rep - 1, rows, width), BF16),
                pltpu.VMEM((n_rep, rows, width), BF16),
                pltpu.VMEM((n_blk, grad_rows, width), F32),
                pltpu.VMEM((n_blk - 1, grad_rows, width), F32),
                pltpu.VMEM((grad_rows, width), BF16),
                pltpu.VMEM((n_rep, grad_rows, width), BF16),
                pltpu.VMEM((n_blk, grad_rows, width), F32),
                dma((8,)),
                dma((2, HALVES, n_blk)),
                dma((2, HALVES, n_blk)),
                dma((n_blk,)),
                dma((n_blk,)),
                dma((2, HALVES, n_rep)),
                dma((2, HALVES, n_rep)),
                dma((HALVES, n_rep)),
                dma((HALVES, n_rep)),
                dma((3, wide)),
                dma((3, wide)),
            ],
            compiler_params=pltpu.CompilerParams(
                collective_id=0, has_side_effects=True, vmem_limit_bytes=64 * 2**20 - 1400 * 2**10
            ),
        )(
            feats.reshape(split),
            tiles,
            col_local,
            tile_count.T,
            w_self,
            w_neigh,
            bias,
            cotangent.reshape(split),
        )
        logits, grad_self, grad_neigh, grad_bias = made
        return logits.reshape(feats.shape), grad_self, grad_neigh, grad_bias

    return jax.shard_map(
        shards,
        mesh=mesh,
        in_specs=(
            P(("group", "blk"), None),
            P(("group", "blk"), None, "rep", None),
            P(("group", "blk"), None),
            P(("group", "blk"), None),
            P(),
            P(),
            P(),
            P(("group", "blk"), None),
        ),
        out_specs=(
            P(("group", "blk"), None),
            P("group", None, None),
            P("group", None, None),
            P("group", None),
        ),
        check_vma=False,
    )
```
